128 devices in a mesh: section: 2 (over core), dev: 64 (over z, y, x).
Axes of the slice: x: 4, y: 4, z: 4, core: 2. Of those that a mesh axis runs over, the one named last changes fastest.
Arguments:
- hidden_rows: bfloat16 [2, 1024, 7168], P('section', 'dev'), may hold values from -6 to 6
- routes: int32 [2, 1024, 8], P('section', 'dev'), may hold values from 0 to 63, all different within a row; in each aligned block of 16 rows (0 to 15, 16 to 31, ..., all dimensions but the last counted through in order) at most 4 rows name the same one
- gate_weights: float32 [2, 1024, 8], P('section', 'dev'), may hold values from 0.05 to 0.5
- gate_proj: bfloat16 [64, 7168, 1024], P('dev', None, 'section'), may hold values from -0.0625 to 0.0625
- up_proj: bfloat16 [64, 7168, 1024], P('dev', None, 'section'), may hold values from -0.0625 to 0.0625
- down_proj: bfloat16 [64, 1024, 7168], P('dev', 'section'), may hold values from -0.1875 to 0.1875
- queries: bfloat16 [2, 128, 128, 576], P('section', 'dev'), may hold values from -50 to 50
- latent_cache: bfloat16 [2, 128, 1024, 576], P('section', 'dev'), may hold values from -6 to 6
- cache_lengths: int32 [2, 128], P('section', 'dev'), may hold values from 128 to 1024, as said below
Outputs:
- moe_out: bfloat16 [2, 1024, 7168], P('section', 'dev')
- attn_out: bfloat16 [2, 128, 128, 512], P('section', 'dev')
The draws below stay inside these ranges and needn't reach their ends.
Inputs may be any that keep to these rules, and one draw needn't show every extreme that they name: `routes`: in each aligned block of 16 rows no expert is named by more than 4 pairs, a bound that some block reaches; a row names 8 different experts. `cache_lengths`: some request has exactly 1024 used slots.
All inputs are finite; a program needn't handle non-finite values.
Results may differ from the reference program's by a relative error of at most 0.011.
Values may be sent and summed in bfloat16 or wider, within the bound.
No kernel may reach another device: no remote copies, remote signals or barrier semaphores. Data moves between devices by JAX's collectives and lax.ppermute only.
A program may use at most 128 MiB of HBM per device.

```python
import math
import jax
import jax.numpy as jnp
import numpy as np
from jax import lax

D = 7168
H = 1024
HEADS = 128
LAT = 512
ROPE = 64
TOP = 8
ROWS_DEV = 16
LEN = 1024
EXPERTS = 64
CAP = 4
TOKENS = 1024
REQS = 128
N_DEV = 64


def shared_latent(key):
    return jax.random.truncated_normal(key, -6.0, 6.0, (2, REQS, LEN, LAT + ROPE), jnp.float32)


def draw_latent_cache(key, part):
    base = shared_latent(key)
    return base.astype(jnp.bfloat16)


def draw_queries(key, part):
    key = jax.random.fold_in(key, 23)
    first_key = jax.random.fold_in(key, 0)
    drawn = jax.random.truncated_normal(first_key, -6.0, 6.0, (2, REQS, HEADS, LAT + ROPE), jnp.float32)
    return drawn.astype(jnp.bfloat16)


def draw_cache_lengths(key, part):
    key = jax.random.fold_in(key, 37)
    lengths = jax.random.randint(key, (2, REQS), LEN // 8, LEN + 1, jnp.int32)
    return lengths.at[0, 0].set(LEN)


def level_of(rng, shape, shards, low, high):
    def one(position, parts):
        draws = jax.random.uniform(jax.random.fold_in(jax.random.fold_in(rng, 6), position), (parts,), jnp.float32, low / len(shards), high / len(shards))
        return jnp.repeat(jnp.exp(draws), shape[position] // parts).reshape((-1,) + (1,) * (len(shape) - position - 1))

    gain = one(*shards[0])
    for cut in shards[1:]:
        gain = gain * one(*cut)
    return gain


def routed_block(stream_key, own, number, rows, amount, top, most, lean):
    order = jax.random.permutation(stream_key, amount)
    heavy_load, usual = load_shares(amount, rows * top, most, lean, True), load_shares(amount, rows * top, most, lean, False)
    places = jnp.arange(amount)

    def named(tallies, rotation):
        used = int((tallies > 0).sum())
        fixed = max(1, used // 4)
        passed = fixed + (places - fixed + rotation * (used - fixed)) % max(1, amount - fixed)
        return jnp.zeros((amount,), jnp.int32).at[order[jnp.where(places < fixed, places, passed)]].set(jnp.asarray(tallies, jnp.int32))

    tallies = jnp.where(number % 4 == 0, named(heavy_load, number // 4), named(usual, number - number // 4 - 1))
    mixed = jax.random.permutation(jax.random.fold_in(own, 3), amount)
    source_of, sink = mixed[0:amount // 2 * 2:2], mixed[1:amount // 2 * 2:2]
    margin = jnp.minimum(tallies[source_of] - 1, most - tallies[sink]) // 2
    margin = jnp.where((source_of == order[0]) | (sink == order[0]) | (tallies[sink] == 0), 0, jnp.maximum(margin, 0))
    passed = jax.random.randint(jax.random.fold_in(own, 4), (amount // 2,), 0, 1 << 20) % (margin + 1)
    tallies = tallies.at[source_of].add(-passed).at[sink].add(passed)
    items = jnp.searchsorted(jnp.cumsum(tallies), jnp.arange(rows * top), side="right").astype(jnp.int32)
    table = items.reshape(top, rows).T
    table = table[jax.random.permutation(jax.random.fold_in(own, 1), rows)]
    rotation = jax.random.randint(jax.random.fold_in(own, 2), (rows, 1), 0, top)
    return jnp.take_along_axis(table, (jnp.arange(top)[None, :] + rotation) % top, axis=1)


def load_shares(number_of, total, reach, skew, full):
    loads = [(1 << 20) // math.isqrt(grade ** skew) + 1 for grade in range(1, number_of + 1)]
    largest = reach if full else min(reach, max(-(-total // number_of), total * loads[0] // sum(loads)))
    least = 1 if total - largest >= number_of - 1 else 0
    given, spare = [largest] + [least] * (number_of - 1), total - largest - least * (number_of - 1)
    while spare > 0:
        free = [i for i in range(1, number_of) if given[i] < largest] or [i for i in range(1, number_of) if given[i] < reach]
        pool, remaining = sum([loads[i] for i in free]), spare
        for i in free:
            addition = min(reach - given[i], max(1, remaining * loads[i] // pool), spare)
            given[i] = given[i] + addition
            spare = spare - addition
    return np.array(given)


def gaussian(own_key, dims, scale, most, cuts=(), held_as=jnp.bfloat16):
    drawn = scale * jax.random.normal(own_key, dims, jnp.float32)
    if cuts:
        drawn = drawn * level_of(own_key, dims, cuts, -0.22, 0.18)
    return jnp.clip(drawn, -most, most).astype(held_as)


def setup_inputs(seed: int = 0) -> dict:
    key_list = jax.random.split(jax.random.key(seed), 10)
    hidden_rows = gaussian(key_list[0], (2, TOKENS, D), 1.0, 6.0, ((0, 2), (1, 64)))
    routes_keys = jax.random.split(jax.random.fold_in(key_list[1], 1), 2 * TOKENS // ROWS_DEV)
    routes_turns = jax.random.permutation(jax.random.fold_in(key_list[1], 3), 2 * TOKENS // ROWS_DEV)
    routes = jax.vmap(lambda own, number: routed_block(jax.random.fold_in(key_list[1], 2), own, number, ROWS_DEV, EXPERTS, TOP, CAP, 2))(routes_keys, routes_turns).reshape((2, TOKENS, TOP))
    gate_weights = jnp.clip(0.05 + 0.45 * jax.random.uniform(key_list[2], (2, TOKENS, TOP), jnp.float32) ** level_of(key_list[2], (2, TOKENS, TOP), ((0, 2), (1, 64)), -0.2, 0.2), 0.05, 0.5)
    gate_proj = gaussian(key_list[3], (EXPERTS, D, H), D ** -0.5, 0.0625, ((0, 64), (2, 2)))
    up_proj = gaussian(key_list[4], (EXPERTS, D, H), D ** -0.5, 0.0625, ((0, 64), (2, 2)))
    down_proj = gaussian(key_list[5], (EXPERTS, H, D), H ** -0.5, 0.1875, ((0, 64), (1, 2)))
    queries = draw_queries(jax.random.fold_in(key_list[9], 71), 0)
    latent_cache = draw_latent_cache(jax.random.fold_in(key_list[9], 71), 0)
    cache_lengths = draw_cache_lengths(jax.random.fold_in(key_list[9], 71), 0)
    return dict(hidden_rows=hidden_rows, routes=routes, gate_weights=gate_weights, gate_proj=gate_proj, up_proj=up_proj, down_proj=down_proj, queries=queries, latent_cache=latent_cache, cache_lengths=cache_lengths)


qk_scale = 192.0 ** -0.5


def block_positions(block_routes):
    flat = block_routes.reshape(-1)
    onehot = (flat[:, None] == jnp.arange(EXPERTS, dtype=jnp.int32)[None, :]).astype(jnp.int32)
    before = jnp.cumsum(onehot, axis=0) - onehot
    return jnp.sum(before * onehot, axis=1).astype(jnp.int32)


def reference(hidden_rows, routes, gate_weights, gate_proj, up_proj, down_proj, queries, latent_cache, cache_lengths):
    rows_all = 2 * N_DEV * ROWS_DEV
    blocks = 2 * N_DEV
    inputs = hidden_rows.reshape(rows_all, D)
    positions = jax.vmap(block_positions)(routes.reshape(blocks, ROWS_DEV, TOP)).reshape(-1)
    expert_ids = routes.reshape(-1).astype(jnp.int32)
    pair_ids = jnp.arange(rows_all * TOP, dtype=jnp.int32)
    row_ids = pair_ids // TOP
    block_ids = row_ids // ROWS_DEV
    column = block_ids * CAP + positions
    table = jnp.full((EXPERTS, blocks * CAP), rows_all, jnp.int32).at[expert_ids, column].set(row_ids)
    weights = jnp.zeros((EXPERTS, blocks * CAP), jnp.float32).at[expert_ids, column].set(gate_weights.reshape(-1))
    padded = jnp.concatenate([inputs, jnp.zeros((1, D), jnp.bfloat16)], axis=0)
    half = H // 2

    def one_expert(total, items):
        indices, gains, w_gate, w_up, w_down = items
        picked = padded[indices]
        gate = jnp.dot(picked, w_gate, preferred_element_type=jnp.float32)
        upper = jnp.dot(picked, w_up, preferred_element_type=jnp.float32)
        hidden = (jax.nn.silu(gate) * upper).astype(jnp.bfloat16)
        first = jnp.dot(hidden[:, :half], w_down[:half], preferred_element_type=jnp.float32).astype(jnp.bfloat16)
        second = jnp.dot(hidden[:, half:], w_down[half:], preferred_element_type=jnp.float32).astype(jnp.bfloat16)
        output = (first.astype(jnp.float32) + second.astype(jnp.float32)).astype(jnp.bfloat16)
        total = total.at[indices].add(gains[:, None] * output.astype(jnp.float32))
        return total, None

    total, unused = lax.scan(one_expert, jnp.zeros((rows_all + 1, D), jnp.float32), (table, weights, gate_proj, up_proj, down_proj))
    moe_out = total[:rows_all].astype(jnp.bfloat16).reshape(2, N_DEV * ROWS_DEV, D)

    query_f = queries.astype(jnp.float32)
    cache_f = latent_cache.astype(jnp.float32)
    scores = jnp.einsum("srhc,srlc->srhl", query_f, cache_f) * qk_scale
    valid = jnp.arange(LEN, dtype=jnp.int32)[None, None, None, :] < cache_lengths[:, :, None, None]
    scores = jnp.where(valid, scores, -jnp.inf)
    peak = jnp.max(scores, axis=-1, keepdims=True)
    expo = jnp.where(valid, jnp.exp(scores - peak), 0.0)
    probs = (expo / jnp.sum(expo, axis=-1, keepdims=True)).astype(jnp.bfloat16)
    attn_out = jnp.einsum("srhl,srlc->srhc", probs.astype(jnp.float32), cache_f[..., :LAT]).astype(jnp.bfloat16)
    return moe_out, attn_out
```

```python
import jax
import jax.numpy as jnp
from jax import lax
from jax.sharding import PartitionSpec as P

LAT = 512
SIDE = 4
CAP = 4
BF16 = jnp.bfloat16
F32 = jnp.float32

qk_scale = 192.0 ** (-0.5)

STRIDE = (16, 4, 1)
ORDERS = ((0, 1, 2), (1, 2, 0), (2, 0, 1))


def shift_along(value, axis, step):
    stride = STRIDE[axis]
    pairs = []
    for source in range(SIDE**3):
        place = (source // stride) % SIDE
        target = source + ((place + step) % SIDE - place) * stride
        pairs.append((source, target))
    return lax.ppermute(value, "dev", pairs)


def swap_sections(value):
    return lax.ppermute(value, "section", [(0, 1), (1, 0)])


def dot32(left, right):
    return jnp.dot(left, right, preferred_element_type=F32)


def attention(queries, cache, lengths):
    scores = jnp.einsum("rhc,rlc->rhl", queries, cache, preferred_element_type=F32) * qk_scale
    slots = cache.shape[1]
    valid = jnp.arange(slots, dtype=jnp.int32)[None, None, :] < lengths[:, None, None]
    scores = jnp.where(valid, scores, -jnp.inf)
    peak = jnp.max(scores, axis=-1, keepdims=True)
    expo = jnp.where(valid, jnp.exp(scores - peak), 0.0)
    probs = (expo / jnp.sum(expo, axis=-1, keepdims=True)).astype(BF16)
    values = cache[:, :, :LAT]
    return jnp.einsum("rhl,rlc->rhc", probs, values, preferred_element_type=F32).astype(BF16)


def plane_tables(order, table, place):
    first, second, last = order
    rows, top = 16, 8
    ks = jnp.arange(SIDE, dtype=jnp.int32)
    at_first = (place[first] - ks) % SIDE
    at_second = (place[second] - ks) % SIDE
    block_dev = (
        at_second[:, None] * STRIDE[second] + at_first[None, :] * STRIDE[first] + place[last] * STRIDE[last]
    ).reshape(-1)
    block_slot = (at_first[None, :] * SIDE + at_second[:, None]).reshape(-1)
    info = table[block_dev]
    routes = info[:, : rows * top].reshape(SIDE * SIDE, rows, top)
    gains = info[:, rows * top :].reshape(SIDE * SIDE, rows, top)
    expert = (
        place[first] * STRIDE[first]
        + place[second] * STRIDE[second]
        + ((place[last] + ks) % SIDE) * STRIDE[last]
    ).astype(F32)
    match = routes[None] == expert[:, None, None, None]
    named = jnp.any(match, axis=-1)
    gain = jnp.sum(jnp.where(match, gains[None], 0.0), axis=-1)
    count = named.astype(jnp.int32)
    position = jnp.cumsum(count, axis=-1) - count
    slot = block_slot[None, :, None] * CAP + position
    slot = jnp.where(named, slot, -1).reshape(SIDE, -1)
    gain = gain.reshape(SIDE, -1)
    wanted = jnp.arange(SIDE * SIDE * CAP, dtype=jnp.int32)
    select = (slot[:, None, :] == wanted[None, :, None]).astype(BF16)
    weigh = jnp.where(slot[:, :, None] == wanted[None, None, :], gain[:, :, None], 0.0)
    return select, weigh


def arrival_order(order, place):
    first, second, last = order
    slots = SIDE**3 * CAP
    index = jnp.arange(slots, dtype=jnp.int32)
    position = index % CAP
    coords = [(index // (CAP * stride)) % SIDE for stride in STRIDE]
    step = (place[last] - coords[last]) % SIDE
    arrival = (step * SIDE * SIDE + coords[first] * SIDE + coords[second]) * CAP + position
    return (arrival[:, None] == index[None, :]).astype(BF16)


def per_device(
    hidden_rows,
    routes,
    gate_weights,
    gate_proj,
    up_proj,
    down_proj,
    queries,
    latent_cache,
    cache_lengths,
):
    inputs = hidden_rows[0]
    width = inputs.shape[1]
    w_gate, w_up, w_down = gate_proj[0], up_proj[0], down_proj[0]
    me = lax.axis_index("dev")
    place = [(me // stride) % SIDE for stride in STRIDE]

    info = jnp.concatenate(
        [routes[0].astype(F32).reshape(1, -1), gate_weights[0].reshape(1, -1)], axis=1
    )
    table = lax.all_gather(info, "dev", axis=0, tiled=True)

    lanes = width // 128
    cuts = [0, (lanes + 2) // 3 * 128, ((lanes + 2) // 3 + (lanes + 1) // 3) * 128, width]
    columns = [slice(cuts[p], cuts[p + 1]) for p in range(3)]

    held = [inputs[:, c] for c in columns]
    for stage in range(2):
        held = [gather_along(held[p], ORDERS[p][stage]) for p in range(3)]

    tables = [plane_tables(ORDERS[p], table, place) for p in range(3)]
    orders = [arrival_order(ORDERS[p], place) for p in range(3)]

    gate, upper = 0.0, 0.0
    for p in range(3):
        picked = [dot32(tables[p][0][k], held[p]).astype(BF16) for k in range(SIDE)]
        arrived = [picked[0]] + [shift_along(picked[k], ORDERS[p][2], k) for k in range(1, SIDE)]
        mine = dot32(orders[p], jnp.concatenate(arrived, axis=0)).astype(BF16)
        both = jnp.concatenate([mine, swap_sections(mine)], axis=0)
        gate = gate + dot32(both, w_gate[columns[p]])
        upper = upper + dot32(both, w_up[columns[p]])
    hidden = (jax.nn.silu(gate) * upper).astype(BF16)

    slots = SIDE**3 * CAP
    out = []
    for p in range(3):
        first, second, last = ORDERS[p]
        theirs = dot32(hidden[slots:], w_down[:, columns[p]]).astype(BF16)
        mine = dot32(hidden[:slots], w_down[:, columns[p]]).astype(BF16)
        total = (mine.astype(F32) + swap_sections(theirs).astype(F32)).astype(BF16)
        leaving = dot32(orders[p].T, total).astype(BF16).reshape(SIDE, slots // SIDE, -1)
        back = [leaving[0]] + [shift_along(leaving[k], last, -k) for k in range(1, SIDE)]
        weigh = tables[p][1]
        high = weigh.astype(BF16)
        low = (weigh - high.astype(F32)).astype(BF16)
        summed = sum(dot32(high[k], back[k]) + dot32(low[k], back[k]) for k in range(SIDE)).astype(BF16)
        for axis in (second, first):
            pieces = summed.reshape(SIDE, summed.shape[0] // SIDE, -1)
            summed = sum(
                [pieces[0].astype(F32)]
                + [shift_along(pieces[k], axis, -k).astype(F32) for k in range(1, SIDE)]
            ).astype(BF16)
        out.append(summed)
    moe_out = jnp.concatenate(out, axis=1)[None]
    attn_out = attention(queries[0], latent_cache[0], cache_lengths[0])[None]
    return (moe_out, attn_out)


def gather_along(value, axis):
    return jnp.concatenate([value] + [shift_along(value, axis, k) for k in range(1, SIDE)], axis=0)


def solution(mesh):
    return jax.shard_map(
        per_device,
        mesh=mesh,
        in_specs=(
            P("section", "dev", None),
            P("section", "dev", None),
            P("section", "dev", None),
            P("dev", None, "section"),
            P("dev", None, "section"),
            P("dev", "section", None),
            P("section", "dev", None, None),
            P("section", "dev", None, None),
            P("section", "dev"),
        ),
        out_specs=(P("section", "dev", None), P("section", "dev", None, None)),
        check_vma=False,
    )
```

```python
import functools

import jax
import jax.numpy as jnp
from jax import lax
from jax.experimental import pallas as pl
from jax.experimental.pallas import tpu as pltpu
from jax.sharding import PartitionSpec as P

LAT = 512
SIDE = 4
CAP = 4
ROWS = 16
TOP = 8
INFO = 128
PLANE = SIDE * SIDE * ROWS
SLOTS = SIDE**3 * CAP
PIECE = SLOTS // SIDE
BF16 = jnp.bfloat16
F32 = jnp.float32
I32 = jnp.int32

qk_scale = 192.0 ** (-0.5)

STRIDE = (16, 4, 1)
ORDERS = ((0, 1, 2), (1, 2, 0), (2, 0, 1))


def shift_along(value, axis, step):
    stride = STRIDE[axis]
    pairs = []
    for source in range(SIDE**3):
        place = (source // stride) % SIDE
        target = source + ((place + step) % SIDE - place) * stride
        pairs.append((source, target))
    return lax.ppermute(value, "dev", pairs)


def swap_sections(value):
    return lax.ppermute(value, "section", [(0, 1), (1, 0)])


def dot32(left, right):
    return jnp.dot(left, right, preferred_element_type=F32)


def attention(queries, cache, lengths):
    scores = jnp.einsum("rhc,rlc->rhl", queries, cache, preferred_element_type=F32) * qk_scale
    slots = cache.shape[1]
    valid = jnp.arange(slots, dtype=I32)[None, None, :] < lengths[:, None, None]
    scores = jnp.where(valid, scores, -jnp.inf)
    peak = jnp.max(scores, axis=-1, keepdims=True)
    expo = jnp.where(valid, jnp.exp(scores - peak), 0.0)
    probs = (expo / jnp.sum(expo, axis=-1, keepdims=True)).astype(BF16)
    values = cache[:, :, :LAT]
    return jnp.einsum("rhl,rlc->rhc", probs, values, preferred_element_type=F32).astype(BF16)


def local_call(body, out, *operands, flops=0, scalars=0):
    specs = [
        pl.BlockSpec(memory_space=pltpu.SMEM if i < scalars else pltpu.VMEM)
        for i in range(len(operands))
    ]
    moved = sum(v.size * v.dtype.itemsize for v in operands) + sum(
        v.size * v.dtype.itemsize for v in out
    )
    return pl.pallas_call(
        body,
        out_shape=out,
        in_specs=specs,
        out_specs=[pl.BlockSpec(memory_space=pltpu.VMEM)] * len(out),
        cost_estimate=pl.CostEstimate(flops=flops, bytes_accessed=moved, transcendentals=0),
        compiler_params=pltpu.CompilerParams(vmem_limit_bytes=24 * 2**20),
    )(*operands)


def shaped(rows, width, dtype=BF16):
    return jax.ShapeDtypeStruct((rows, width), dtype)


def tiles(width, step=512):
    return [slice(lo, min(lo + step, width)) for lo in range(0, width, step)]


def iota(shape, dim):
    return lax.broadcasted_iota(I32, shape, dim)


def split_body(cuts, rows_ref, info_ref, *out_refs):
    for p, ref in enumerate(out_refs):
        width = cuts[p + 1] - cuts[p]
        ref[:, :width] = rows_ref[:, cuts[p] : cuts[p + 1]]
        ref[:, width:] = info_ref[...]


def stack_body(*refs):
    out = refs[-1]
    rows = refs[0].shape[0]
    for k, ref in enumerate(refs[:-1]):
        out[k * rows : (k + 1) * rows, :] = ref[...]


def select_body(order, place_ref, *refs):
    held, outs, high_ref, low_ref = refs[:SIDE], refs[SIDE : 2 * SIDE], refs[-2], refs[-1]
    first, second, last = order
    width = outs[0].shape[1]
    info = jnp.concatenate([ref[:, width:] for ref in held], axis=0).astype(F32)
    lane = iota((PLANE, INFO), 1)
    gains = pltpu.roll(info, INFO - TOP, 1) + pltpu.roll(info, INFO - 2 * TOP, 1)
    row = iota((PLANE, 1), 0)
    at_first = lax.rem(place_ref[first] + SIDE - lax.rem(lax.div(row, ROWS), SIDE), SIDE)
    at_second = lax.rem(place_ref[second] + SIDE - lax.div(row, ROWS * SIDE), SIDE)
    block = at_first * SIDE + at_second
    base = place_ref[first] * STRIDE[first] + place_ref[second] * STRIDE[second]
    named, gain = [], []
    marks = jnp.zeros((PLANE, INFO), F32)
    for j in range(SIDE):
        expert = (base + lax.rem(place_ref[last] + j, SIDE) * STRIDE[last]).astype(F32)
        match = (info == expert) & (lane < TOP)
        one = jnp.sum(jnp.where(match, 1.0, 0.0), axis=1, keepdims=True)
        named.append(one)
        gain.append(jnp.sum(jnp.where(match, gains, 0.0), axis=1, keepdims=True))
        marks = jnp.where(lane == j, one, marks)
    left, right = iota((PLANE, PLANE), 0), iota((PLANE, PLANE), 1)
    earlier = (lax.div(left, ROWS) == lax.div(right, ROWS)) & (right < left)
    position = dot32(jnp.where(earlier, 1.0, 0.0).astype(BF16), marks.astype(BF16)).astype(I32)
    select = jnp.zeros((PLANE, SLOTS), F32)
    weigh = jnp.zeros((PLANE, SLOTS), F32)
    for j in range(SIDE):
        slot = block * CAP + position[:, j : j + 1] + j * PIECE
        hit = (right == slot) & (named[j] > 0.5)
        select = jnp.where(hit, 1.0, select)
        weigh = jnp.where(hit, gain[j], weigh)
    high = weigh.astype(BF16)
    high_ref[...] = high
    low_ref[...] = (weigh - high.astype(F32)).astype(BF16)
    select = select.T.astype(BF16)
    for cols in tiles(width):
        rows = jnp.concatenate([ref[:, cols] for ref in held], axis=0)
        picked = dot32(select, rows).astype(BF16)
        for j in range(SIDE):
            outs[j][:, cols] = picked[j * PIECE : (j + 1) * PIECE]


def arrival(order, place_ref, transposed):
    first, second, last = order
    index = iota((SLOTS, SLOTS), 1 if transposed else 0)
    other = iota((SLOTS, SLOTS), 0 if transposed else 1)
    position = lax.rem(index, CAP)
    coords = [lax.rem(lax.div(index, CAP * stride), SIDE) for stride in STRIDE]
    step = lax.rem(place_ref[last] + SIDE - coords[last], SIDE)
    where = ((step * SIDE + coords[first]) * SIDE + coords[second]) * CAP + position
    return jnp.where(where == other, 1.0, 0.0).astype(BF16)


def arrive_body(order, place_ref, *refs):
    pieces, out = refs[:SIDE], refs[-1]
    turn = arrival(order, place_ref, False)
    for cols in tiles(out.shape[1]):
        rows = jnp.concatenate([ref[:, cols] for ref in pieces], axis=0)
        out[:, cols] = dot32(turn, rows).astype(BF16)


def leave_body(order, place_ref, mine_ref, other_ref, *outs):
    turn = arrival(order, place_ref, True)
    for cols in tiles(mine_ref.shape[1]):
        total = (mine_ref[:, cols].astype(F32) + other_ref[:, cols].astype(F32)).astype(BF16)
        turned = dot32(turn, total).astype(BF16)
        for j in range(SIDE):
            outs[j][:, cols] = turned[j * PIECE : (j + 1) * PIECE]


def combine_body(high_ref, low_ref, *refs):
    pieces, outs = refs[:SIDE], refs[SIDE:]
    weigh = jnp.concatenate([high_ref[...], low_ref[...]], axis=1)
    rows = PLANE // SIDE
    for cols in tiles(pieces[0].shape[1]):
        value = jnp.concatenate([ref[:, cols] for ref in pieces] * 2, axis=0)
        summed = dot32(weigh, value).astype(BF16)
        for k in range(SIDE):
            outs[k][:, cols] = summed[k * rows : (k + 1) * rows]


def add_body(*refs):
    pieces, outs = refs[:SIDE], refs[SIDE:]
    for cols in tiles(pieces[0].shape[1]):
        total = sum(ref[:, cols].astype(F32) for ref in pieces).astype(BF16)
        for k in range(SIDE):
            outs[k][:, cols] = total[k * ROWS : (k + 1) * ROWS]


def finish_body(cuts, *refs):
    out = refs[-1]
    for p in range(len(ORDERS)):
        pieces = refs[p * SIDE : (p + 1) * SIDE]
        out[:, cuts[p] : cuts[p + 1]] = sum(ref[...].astype(F32) for ref in pieces).astype(BF16)


def per_device(
    hidden_rows,
    routes,
    gate_weights,
    gate_proj,
    up_proj,
    down_proj,
    queries,
    latent_cache,
    cache_lengths,
):
    inputs = hidden_rows[0]
    width = inputs.shape[1]
    w_gate, w_up, w_down = gate_proj[0], up_proj[0], down_proj[0]
    me = lax.axis_index("dev")
    place = jnp.stack([(me // stride) % SIDE for stride in STRIDE]).astype(I32)

    gains = gate_weights[0]
    high = gains.astype(BF16)
    low = (gains - high.astype(F32)).astype(BF16)
    info = jnp.concatenate(
        [routes[0].astype(BF16), high, low, jnp.zeros((ROWS, INFO - 3 * TOP), BF16)], axis=1
    )

    lanes = width // 128
    cuts = (0, (lanes + 2) // 3 * 128, ((lanes + 2) // 3 + (lanes + 1) // 3) * 128, width)
    sizes = [cuts[p + 1] - cuts[p] for p in range(3)]
    parts = range(3)

    started = local_call(
        functools.partial(split_body, cuts), [shaped(ROWS, n + INFO) for n in sizes], inputs, info
    )
    gathered = []
    for p in parts:
        pieces = [started[p]] + [shift_along(started[p], ORDERS[p][0], k) for k in (1, 2, 3)]
        gathered += local_call(stack_body, [shaped(ROWS * SIDE, sizes[p] + INFO)], *pieces)
    picked, weighs = [], []
    for p in parts:
        pieces = [gathered[p]] + [shift_along(gathered[p], ORDERS[p][1], k) for k in (1, 2, 3)]
        result = local_call(
            functools.partial(select_body, ORDERS[p]),
            [shaped(PIECE, sizes[p])] * SIDE + [shaped(PLANE, SLOTS)] * 2,
            place,
            *pieces,
            flops=2 * PLANE * SLOTS * sizes[p],
            scalars=1,
        )
        picked.append(result[:SIDE])
        weighs.append(result[SIDE:])
    mine, other = [], []
    for p in parts:
        pieces = [picked[p][0]] + [shift_along(picked[p][k], ORDERS[p][2], k) for k in (1, 2, 3)]
        mine += local_call(
            functools.partial(arrive_body, ORDERS[p]),
            [shaped(SLOTS, sizes[p])],
            place,
            *pieces,
            flops=2 * SLOTS * SLOTS * sizes[p],
            scalars=1,
        )
        other.append(swap_sections(mine[p]))

    def hidden_of(blocks):
        gate, upper = 0.0, 0.0
        for p in parts:
            gate = gate + dot32(blocks[p], w_gate[cuts[p] : cuts[p + 1]])
            upper = upper + dot32(blocks[p], w_up[cuts[p] : cuts[p + 1]])
        return (jax.nn.silu(gate) * upper).astype(BF16)

    hidden_mine, hidden_other = hidden_of(mine), hidden_of(other)

    last = []
    for p in parts:
        first, second, third = ORDERS[p]
        down = w_down[:, cuts[p] : cuts[p + 1]]
        returned = swap_sections(dot32(hidden_other, down).astype(BF16))
        kept = dot32(hidden_mine, down).astype(BF16)
        leaving = local_call(
            functools.partial(leave_body, ORDERS[p]),
            [shaped(PIECE, sizes[p])] * SIDE,
            place,
            kept,
            returned,
            flops=2 * SLOTS * SLOTS * sizes[p],
            scalars=1,
        )
        back = [leaving[0]] + [shift_along(leaving[k], third, -k) for k in (1, 2, 3)]
        summed = local_call(
            combine_body,
            [shaped(PLANE // SIDE, sizes[p])] * SIDE,
            *weighs[p],
            *back,
            flops=4 * PLANE * SLOTS * sizes[p],
        )
        back = [summed[0]] + [shift_along(summed[k], second, -k) for k in (1, 2, 3)]
        summed = local_call(add_body, [shaped(ROWS, sizes[p])] * SIDE, *back)
        last += [summed[0]] + [shift_along(summed[k], first, -k) for k in (1, 2, 3)]
    moe_out = local_call(functools.partial(finish_body, cuts), [shaped(ROWS, width)], *last)[0]
    attn_out = attention(queries[0], latent_cache[0], cache_lengths[0])
    return (moe_out[None], attn_out[None])


def solution(mesh):
    return jax.shard_map(
        per_device,
        mesh=mesh,
        in_specs=(
            P("section", "dev", None),
            P("section", "dev", None),
            P("section", "dev", None),
            P("dev", None, "section"),
            P("dev", None, "section"),
            P("dev", "section", None),
            P("section", "dev", None, None),
            P("section", "dev", None, None),
            P("section", "dev"),
        ),
        out_specs=(P("section", "dev", None), P("section", "dev", None, None)),
        check_vma=False,
    )
```

```python
import jax
import jax.numpy as jnp
from jax import lax
from jax.experimental import pallas as pl
from jax.experimental.pallas import tpu as pltpu
from jax.sharding import PartitionSpec as P

LAT = 512
SIDE = 4
CAP = 4
ROWS = 16
TOP = 8
SLOTS = SIDE**3 * CAP
BF16 = jnp.bfloat16
F32 = jnp.float32
I32 = jnp.int32

qk_scale = 192.0 ** (-0.5)

def swap_sections(value):
    return lax.ppermute(value, "section", [(0, 1), (1, 0)])


def dot32(left, right):
    return jnp.dot(left, right, preferred_element_type=F32)


def attention(queries, cache, lengths):
    scores = jnp.einsum("rhc,rlc->rhl", queries, cache, preferred_element_type=F32) * qk_scale
    slots = cache.shape[1]
    valid = jnp.arange(slots, dtype=I32)[None, None, :] < lengths[:, None, None]
    scores = jnp.where(valid, scores, -jnp.inf)
    peak = jnp.max(scores, axis=-1, keepdims=True)
    expo = jnp.where(valid, jnp.exp(scores - peak), 0.0)
    probs = (expo / jnp.sum(expo, axis=-1, keepdims=True)).astype(BF16)
    values = cache[:, :, :LAT]
    return jnp.einsum("rhl,rlc->rhc", probs, values, preferred_element_type=F32).astype(BF16)


def local_call(body, out, *operands, flops=0, scalars=0):
    specs = [
        pl.BlockSpec(memory_space=pltpu.SMEM if i < scalars else pltpu.VMEM)
        for i in range(len(operands))
    ]
    moved = sum(v.size * v.dtype.itemsize for v in operands) + sum(
        v.size * v.dtype.itemsize for v in out
    )
    return pl.pallas_call(
        body,
        out_shape=out,
        in_specs=specs,
        out_specs=[pl.BlockSpec(memory_space=pltpu.VMEM)] * len(out),
        cost_estimate=pl.CostEstimate(flops=flops, bytes_accessed=moved, transcendentals=0),
        compiler_params=pltpu.CompilerParams(vmem_limit_bytes=24 * 2**20),
    )(*operands)


def shaped(rows, width, dtype=BF16):
    return jax.ShapeDtypeStruct((rows, width), dtype)


def tiles(width, step=512):
    return [slice(lo, min(lo + step, width)) for lo in range(0, width, step)]


def iota(shape, dim):
    return lax.broadcasted_iota(I32, shape, dim)


def select_body(routes_ref, gains_ref, rows_ref, out_ref, weigh_ref):
    quarter = rows_ref.shape[1] // SIDE
    shape = (SIDE * ROWS, out_ref.shape[0])
    left, right = iota(shape, 0), iota(shape, 1)
    expert = lax.div(right, SIDE * CAP)
    routes = jnp.concatenate([routes_ref[...]] * SIDE, axis=0)
    gains = jnp.concatenate([gains_ref[...]] * SIDE, axis=0)
    named = jnp.zeros(shape, F32)
    weigh = jnp.zeros(shape, F32)
    for k in range(TOP):
        match = routes[:, k : k + 1] == expert
        named = jnp.where(match, 1.0, named)
        weigh = jnp.where(match, gains[:, k : k + 1], weigh)
    square = (SIDE * ROWS, SIDE * ROWS)
    row, column = iota(square, 0), iota(square, 1)
    earlier = (lax.div(row, ROWS) == lax.div(column, ROWS)) & (column < row)
    position = dot32(jnp.where(earlier, 1.0, 0.0).astype(BF16), named.astype(BF16)).astype(I32)
    hit = (
        (named > 0.5)
        & (position == lax.rem(right, CAP))
        & (lax.rem(lax.div(right, CAP), SIDE) == lax.div(left, ROWS))
    )
    weigh = jnp.where(hit, weigh, 0.0)
    high = weigh.astype(BF16)
    weigh_ref[: SIDE * ROWS, :] = high
    weigh_ref[SIDE * ROWS :, :] = (weigh - high.astype(F32)).astype(BF16)
    select = jnp.where(hit, 1.0, 0.0).T.astype(BF16)
    for cols in tiles(quarter, 256):
        rows = jnp.concatenate(
            [
                rows_ref[:, c * quarter + cols.start : c * quarter + cols.stop]
                for c in range(SIDE)
            ],
            axis=0,
        )
        out_ref[:, cols] = dot32(select, rows).astype(BF16)


def quarters_first(transposed):
    rows = SIDE * SIDE * ROWS
    out = iota((rows, rows), 1 if transposed else 0)
    given = iota((rows, rows), 0 if transposed else 1)
    group = SIDE * SIDE * CAP
    quarter, source = lax.div(out, group), lax.div(lax.rem(out, group), CAP)
    where = (source * SIDE + quarter) * CAP + lax.rem(out, CAP)
    return jnp.where(where == given, 1.0, 0.0).astype(BF16)


def arrive_body(raw_ref, out_ref):
    quarter = raw_ref.shape[1]
    turn = quarters_first(False)
    rows, group = turn.shape[0], turn.shape[0] // SIDE
    for g in range(raw_ref.shape[0] // rows):
        for cols in tiles(quarter, 256):
            turned = dot32(turn, raw_ref[g * rows : (g + 1) * rows, cols]).astype(BF16)
            for c in range(SIDE):
                out_ref[
                    g * group : (g + 1) * group, c * quarter + cols.start : c * quarter + cols.stop
                ] = turned[c * group : (c + 1) * group]


def leave_body(*refs):
    halves = len(refs) // 2
    mine, other, out_ref = refs[:halves], refs[halves : 2 * halves], refs[-1]
    quarter = out_ref.shape[1]
    turn = quarters_first(True)
    rows, group = turn.shape[0], turn.shape[0] // SIDE
    width = mine[0].shape[1]
    for g in range(out_ref.shape[0] // rows):
        for cols in tiles(quarter, 256):
            total = []
            for c in range(SIDE):
                h, at = divmod(c * quarter + cols.start, width)
                span = slice(at, at + cols.stop - cols.start)
                keep = slice(g * group, (g + 1) * group)
                total.append(
                    (mine[h][keep, span].astype(F32) + other[h][keep, span].astype(F32)).astype(BF16)
                )
            total = jnp.concatenate(total, axis=0)
            out_ref[g * rows : (g + 1) * rows, cols] = dot32(turn, total).astype(BF16)


def combine_body(weigh_ref, raw_ref, out_ref):
    quarter = raw_ref.shape[1]
    half = SIDE * ROWS
    for cols in tiles(quarter, 256):
        both = dot32(weigh_ref[...], raw_ref[:, cols])
        summed = (both[:half] + both[half:]).astype(BF16)
        for c in range(SIDE):
            out_ref[:, c * quarter + cols.start : c * quarter + cols.stop] = summed[
                c * ROWS : (c + 1) * ROWS
            ]


def per_device(
    hidden_rows,
    routes,
    gate_weights,
    gate_proj,
    up_proj,
    down_proj,
    queries,
    latent_cache,
    cache_lengths,
):
    inputs = hidden_rows[0]
    width = inputs.shape[1]
    w_gate, w_up, w_down = gate_proj[0], up_proj[0], down_proj[0]
    raw_rows, quarter = SLOTS * SIDE, width // SIDE

    outgoing, weigh = local_call(
        select_body,
        [shaped(raw_rows, quarter), shaped(2 * SIDE * ROWS, raw_rows)],
        routes[0],
        gate_weights[0],
        inputs,
        flops=2 * raw_rows * SIDE * ROWS * quarter,
    )
    raw = lax.all_to_all(outgoing, "dev", 0, 0, tiled=True)
    raw_other = swap_sections(raw)

    def hidden_of(value):
        block = local_call(
            arrive_body, [shaped(SLOTS, width)], value, flops=2 * SLOTS * SLOTS * width
        )[0]
        gate = dot32(block, w_gate)
        upper = dot32(block, w_up)
        return (jax.nn.silu(gate) * upper).astype(BF16)

    hidden_mine = hidden_of(raw)
    hidden_other = hidden_of(raw_other)
    halves = [w_down[:, : width // 2], w_down[:, width // 2 :]]
    returned = [swap_sections(dot32(hidden_other, w).astype(BF16)) for w in halves]
    kept = [dot32(hidden_mine, w).astype(BF16) for w in halves]
    leaving = local_call(
        leave_body,
        [shaped(raw_rows, quarter)],
        *kept,
        *returned,
        flops=2 * SLOTS * SLOTS * width,
    )[0]
    back = lax.all_to_all(leaving, "dev", 0, 0, tiled=True)
    moe_out = local_call(
        combine_body,
        [shaped(ROWS, width)],
        weigh,
        back,
        flops=4 * raw_rows * SIDE * ROWS * quarter,
    )[0]
    attn_out = attention(queries[0], latent_cache[0], cache_lengths[0])
    return (moe_out[None], attn_out[None])


def solution(mesh):
    return jax.shard_map(
        per_device,
        mesh=mesh,
        in_specs=(
            P("section", "dev", None),
            P("section", "dev", None),
            P("section", "dev", None),
            P("dev", None, "section"),
            P("dev", None, "section"),
            P("dev", "section", None),
            P("section", "dev", None, None),
            P("section", "dev", None, None),
            P("section", "dev"),
        ),
        out_specs=(P("section", "dev", None), P("section", "dev", None, None)),
        check_vma=False,
    )
```

```python
import jax
import jax.numpy as jnp
from jax import lax
from jax.experimental import pallas as pl
from jax.experimental.pallas import tpu as pltpu
from jax.sharding import PartitionSpec as P

LAT = 512
SIDE = 4
CAP = 4
ROWS = 16
TOP = 8
SLOTS = SIDE**3 * CAP
BF16 = jnp.bfloat16
F32 = jnp.float32
I32 = jnp.int32

qk_scale = 192.0 ** (-0.5)

def swap_sections(value):
    return lax.ppermute(value, "section", [(0, 1), (1, 0)])


def dot32(left, right):
    return jnp.dot(left, right, preferred_element_type=F32)


def attention(queries, cache, lengths):
    scores = jnp.einsum("rhc,rlc->rhl", queries, cache, preferred_element_type=F32) * qk_scale
    slots = cache.shape[1]
    valid = jnp.arange(slots, dtype=I32)[None, None, :] < lengths[:, None, None]
    scores = jnp.where(valid, scores, -jnp.inf)
    peak = jnp.max(scores, axis=-1, keepdims=True)
    expo = jnp.where(valid, jnp.exp(scores - peak), 0.0)
    probs = (expo / jnp.sum(expo, axis=-1, keepdims=True)).astype(BF16)
    values = cache[:, :, :LAT]
    return jnp.einsum("rhl,rlc->rhc", probs, values, preferred_element_type=F32).astype(BF16)


def local_call(body, out, *operands, flops=0, scalars=0):
    specs = [
        pl.BlockSpec(memory_space=pltpu.SMEM if i < scalars else pltpu.VMEM)
        for i in range(len(operands))
    ]
    moved = sum(v.size * v.dtype.itemsize for v in operands) + sum(
        v.size * v.dtype.itemsize for v in out
    )
    return pl.pallas_call(
        body,
        out_shape=out,
        in_specs=specs,
        out_specs=[pl.BlockSpec(memory_space=pltpu.VMEM)] * len(out),
        cost_estimate=pl.CostEstimate(flops=flops, bytes_accessed=moved, transcendentals=0),
        compiler_params=pltpu.CompilerParams(vmem_limit_bytes=16 * 2**20),
    )(*operands)


def shaped(rows, width, dtype=BF16):
    return jax.ShapeDtypeStruct((rows, width), dtype)


def tiles(width, step=512):
    return [slice(lo, min(lo + step, width)) for lo in range(0, width, step)]


def iota(shape, dim):
    return lax.broadcasted_iota(I32, shape, dim)


def select_body(routes_ref, gains_ref, rows_ref, out_ref, weigh_ref):
    quarter = rows_ref.shape[1] // SIDE
    shape = (out_ref.shape[0], SIDE * ROWS)
    left, right = iota(shape, 0), iota(shape, 1)
    expert = lax.div(left, SIDE * CAP)
    routes = jnp.concatenate([routes_ref[...]] * SIDE, axis=1)
    gains = jnp.concatenate([gains_ref[...]] * SIDE, axis=1)
    named = jnp.zeros(shape, F32)
    weigh = jnp.zeros(shape, F32)
    for k in range(TOP):
        match = routes[k : k + 1, :] == expert
        named = jnp.where(match, 1.0, named)
        weigh = jnp.where(match, gains[k : k + 1, :], weigh)
    square = (SIDE * ROWS, SIDE * ROWS)
    row, column = iota(square, 0), iota(square, 1)
    earlier = (lax.div(row, ROWS) == lax.div(column, ROWS)) & (row < column)
    position = dot32(named.astype(BF16), jnp.where(earlier, 1.0, 0.0).astype(BF16)).astype(I32)
    hit = (
        (named > 0.5)
        & (position == lax.rem(left, CAP))
        & (lax.rem(lax.div(left, CAP), SIDE) == lax.div(right, ROWS))
    )
    weigh = jnp.where(hit, weigh, 0.0)
    high = weigh.astype(BF16).astype(F32)
    weigh_ref[: SIDE * ROWS, :] = high.T.astype(BF16)
    weigh_ref[SIDE * ROWS :, :] = (weigh - high).T.astype(BF16)
    select = jnp.where(hit, 1.0, 0.0).astype(BF16)
    for cols in tiles(quarter, 256):
        rows = jnp.concatenate(
            [
                rows_ref[:, c * quarter + cols.start : c * quarter + cols.stop]
                for c in range(SIDE)
            ],
            axis=0,
        )
        out_ref[:, cols] = dot32(select, rows).astype(BF16)


def quarters_first(transposed):
    rows = SIDE * SIDE * ROWS
    out = iota((rows, rows), 1 if transposed else 0)
    given = iota((rows, rows), 0 if transposed else 1)
    group = SIDE * SIDE * CAP
    quarter, source = lax.div(out, group), lax.div(lax.rem(out, group), CAP)
    where = (source * SIDE + quarter) * CAP + lax.rem(out, CAP)
    return jnp.where(where == given, 1.0, 0.0).astype(BF16)


def arrive_body(raw_ref, out_ref):
    quarter = raw_ref.shape[1]
    turn = quarters_first(False)
    rows, group = turn.shape[0], turn.shape[0] // SIDE
    for g in range(raw_ref.shape[0] // rows):
        for cols in tiles(quarter, 256):
            turned = dot32(turn, raw_ref[g * rows : (g + 1) * rows, cols]).astype(BF16)
            for c in range(SIDE):
                out_ref[
                    g * group : (g + 1) * group, c * quarter + cols.start : c * quarter + cols.stop
                ] = turned[c * group : (c + 1) * group]


def leave_body(*refs):
    halves = len(refs) // 2
    mine, other, out_ref = refs[:halves], refs[halves : 2 * halves], refs[-1]
    quarter = out_ref.shape[1]
    turn = quarters_first(True)
    rows, group = turn.shape[0], turn.shape[0] // SIDE
    width = mine[0].shape[1]
    for g in range(out_ref.shape[0] // rows):
        for cols in tiles(quarter, 256):
            total = []
            for c in range(SIDE):
                h, at = divmod(c * quarter + cols.start, width)
                span = slice(at, at + cols.stop - cols.start)
                keep = slice(g * group, (g + 1) * group)
                total.append(
                    (mine[h][keep, span].astype(F32) + other[h][keep, span].astype(F32)).astype(BF16)
                )
            total = jnp.concatenate(total, axis=0)
            out_ref[g * rows : (g + 1) * rows, cols] = dot32(turn, total).astype(BF16)


def combine_body(weigh_ref, raw_ref, out_ref):
    quarter = raw_ref.shape[1]
    half = SIDE * ROWS
    for cols in tiles(quarter, 256):
        both = dot32(weigh_ref[...], raw_ref[:, cols])
        summed = (both[:half] + both[half:]).astype(BF16)
        for c in range(SIDE):
            out_ref[:, c * quarter + cols.start : c * quarter + cols.stop] = summed[
                c * ROWS : (c + 1) * ROWS
            ]


def per_device(
    hidden_rows,
    routes,
    gate_weights,
    gate_proj,
    up_proj,
    down_proj,
    queries,
    latent_cache,
    cache_lengths,
):
    inputs = hidden_rows[0]
    width = inputs.shape[1]
    w_gate, w_up, w_down = gate_proj[0], up_proj[0], down_proj[0]
    raw_rows, quarter = SLOTS * SIDE, width // SIDE

    outgoing, weigh = local_call(
        select_body,
        [shaped(raw_rows, quarter), shaped(2 * SIDE * ROWS, raw_rows)],
        routes[0].T,
        gate_weights[0].T,
        inputs,
        flops=2 * raw_rows * SIDE * ROWS * quarter,
    )
    raw = lax.all_to_all(outgoing, "dev", 0, 0, tiled=True)
    raw, *others = lax.optimization_barrier(
        (raw, swap_sections(w_gate), swap_sections(w_up), swap_sections(w_down))
    )
    block = local_call(arrive_body, [shaped(SLOTS, width)], raw, flops=2 * SLOTS * SLOTS * width)[0]
    partials = []
    for gate_half, up_half, down_half in (
        (w_gate, w_up, w_down),
        others,
    ):
        gate = dot32(block, gate_half)
        upper = dot32(block, up_half)
        hidden = lax.optimization_barrier((jax.nn.silu(gate) * upper).astype(BF16))
        partials += [
            dot32(hidden, down_half[:, span]).astype(BF16)
            for span in (slice(0, width // 2), slice(width // 2, width))
        ]
    leaving = local_call(
        leave_body,
        [shaped(raw_rows, quarter)],
        *partials,
        flops=2 * SLOTS * SLOTS * width,
    )[0]
    back = lax.all_to_all(leaving, "dev", 0, 0, tiled=True)
    moe_out = local_call(
        combine_body,
        [shaped(ROWS, width)],
        weigh,
        back,
        flops=4 * raw_rows * SIDE * ROWS * quarter,
    )[0]
    attn_out = attention(queries[0], latent_cache[0], cache_lengths[0])
    return (moe_out[None], attn_out[None])


def solution(mesh):
    return jax.shard_map(
        per_device,
        mesh=mesh,
        in_specs=(
            P("section", "dev", None),
            P("section", "dev", None),
            P("section", "dev", None),
            P("dev", None, "section"),
            P("dev", None, "section"),
            P("dev", "section", None),
            P("section", "dev", None, None),
            P("section", "dev", None, None),
            P("section", "dev"),
        ),
        out_specs=(P("section", "dev", None), P("section", "dev", None, None)),
        check_vma=False,
    )
```

```python
import jax
import jax.numpy as jnp
from jax import lax
from jax.experimental import pallas as pl
from jax.experimental.pallas import tpu as pltpu
from jax.sharding import PartitionSpec as P

LAT = 512
SIDE = 4
CAP = 4
ROWS = 16
TOP = 8
SLOTS = SIDE**3 * CAP
BF16 = jnp.bfloat16
F32 = jnp.float32
I32 = jnp.int32

qk_scale = 192.0 ** (-0.5)

def swap_sections(value):
    return lax.ppermute(value, "section", [(0, 1), (1, 0)])


def dot32(left, right):
    return jnp.dot(left, right, preferred_element_type=F32)


def attention_body(lengths_ref, queries_ref, cache_ref, out_ref):
    for r in range(queries_ref.shape[0]):
        heads = queries_ref[r].astype(F32).T.astype(BF16)
        scores = dot32(heads, cache_ref[r]) * qk_scale
        valid = iota(scores.shape, 1) < lengths_ref[r]
        scores = jnp.where(valid, scores, -jnp.inf)
        peak = jnp.max(scores, axis=1, keepdims=True)
        expo = jnp.where(valid, jnp.exp(scores - peak), 0.0)
        probs = expo / jnp.sum(expo, axis=1, keepdims=True)
        out_ref[r] = dot32(cache_ref[r, :LAT, :], probs.T.astype(BF16)).T.astype(BF16)


def attention(queries, cache, lengths):
    return local_call(
        attention_body,
        [jax.ShapeDtypeStruct((*queries.shape[:2], LAT), BF16)],
        lengths,
        queries.transpose(0, 2, 1),
        cache.transpose(0, 2, 1),
        flops=4 * queries.size * cache.shape[1],
        scalars=1,
    )[0]


def local_call(body, out, *operands, flops=0, scalars=0):
    specs = [
        pl.BlockSpec(memory_space=pltpu.SMEM if i < scalars else pltpu.VMEM)
        for i in range(len(operands))
    ]
    moved = sum(v.size * v.dtype.itemsize for v in operands) + sum(
        v.size * v.dtype.itemsize for v in out
    )
    return pl.pallas_call(
        body,
        out_shape=out,
        in_specs=specs,
        out_specs=[pl.BlockSpec(memory_space=pltpu.VMEM)] * len(out),
        cost_estimate=pl.CostEstimate(flops=flops, bytes_accessed=moved, transcendentals=0),
        compiler_params=pltpu.CompilerParams(vmem_limit_bytes=16 * 2**20),
    )(*operands)


def shaped(rows, width, dtype=BF16):
    return jax.ShapeDtypeStruct((rows, width), dtype)


def tiles(width, step=512):
    return [slice(lo, min(lo + step, width)) for lo in range(0, width, step)]


def iota(shape, dim):
    return lax.broadcasted_iota(I32, shape, dim)


def select_body(routes_ref, gains_ref, rows_ref, out_ref, weigh_ref):
    quarter = rows_ref.shape[1] // SIDE
    shape = (out_ref.shape[0], SIDE * ROWS)
    left, right = iota(shape, 0), iota(shape, 1)
    expert = lax.div(left, SIDE * CAP)
    routes = jnp.concatenate([routes_ref[...]] * SIDE, axis=1)
    gains = jnp.concatenate([gains_ref[...]] * SIDE, axis=1)
    named = jnp.zeros(shape, F32)
    weigh = jnp.zeros(shape, F32)
    for k in range(TOP):
        match = routes[k : k + 1, :] == expert
        named = jnp.where(match, 1.0, named)
        weigh = jnp.where(match, gains[k : k + 1, :], weigh)
    square = (SIDE * ROWS, SIDE * ROWS)
    row, column = iota(square, 0), iota(square, 1)
    earlier = (lax.div(row, ROWS) == lax.div(column, ROWS)) & (row < column)
    position = dot32(named.astype(BF16), jnp.where(earlier, 1.0, 0.0).astype(BF16)).astype(I32)
    hit = (
        (named > 0.5)
        & (position == lax.rem(left, CAP))
        & (lax.rem(lax.div(left, CAP), SIDE) == lax.div(right, ROWS))
    )
    weigh = jnp.where(hit, weigh, 0.0)
    high = weigh.astype(BF16).astype(F32)
    weigh_ref[: SIDE * ROWS, :] = high.T.astype(BF16)
    weigh_ref[SIDE * ROWS :, :] = (weigh - high).T.astype(BF16)
    select = jnp.where(hit, 1.0, 0.0).astype(BF16)
    for cols in tiles(quarter, 256):
        rows = jnp.concatenate(
            [
                rows_ref[:, c * quarter + cols.start : c * quarter + cols.stop]
                for c in range(SIDE)
            ],
            axis=0,
        )
        out_ref[:, cols] = dot32(select, rows).astype(BF16)


def quarters_first(transposed):
    rows = SIDE * SIDE * ROWS
    out = iota((rows, rows), 1 if transposed else 0)
    given = iota((rows, rows), 0 if transposed else 1)
    group = SIDE * SIDE * CAP
    quarter, source = lax.div(out, group), lax.div(lax.rem(out, group), CAP)
    where = (source * SIDE + quarter) * CAP + lax.rem(out, CAP)
    return jnp.where(where == given, 1.0, 0.0).astype(BF16)


def arrive_body(raw_ref, out_ref):
    quarter = raw_ref.shape[1]
    turn = quarters_first(False)
    rows, group = turn.shape[0], turn.shape[0] // SIDE
    for g in range(raw_ref.shape[0] // rows):
        for cols in tiles(quarter, 256):
            turned = dot32(turn, raw_ref[g * rows : (g + 1) * rows, cols]).astype(BF16)
            for c in range(SIDE):
                out_ref[
                    g * group : (g + 1) * group, c * quarter + cols.start : c * quarter + cols.stop
                ] = turned[c * group : (c + 1) * group]


def leave_body(*refs):
    halves = len(refs) // 2
    mine, other, out_ref = refs[:halves], refs[halves : 2 * halves], refs[-1]
    quarter = out_ref.shape[1]
    turn = quarters_first(True)
    rows, group = turn.shape[0], turn.shape[0] // SIDE
    width = mine[0].shape[1]
    for g in range(out_ref.shape[0] // rows):
        for cols in tiles(quarter, 256):
            total = []
            for c in range(SIDE):
                h, at = divmod(c * quarter + cols.start, width)
                span = slice(at, at + cols.stop - cols.start)
                keep = slice(g * group, (g + 1) * group)
                total.append(
                    (mine[h][keep, span].astype(F32) + other[h][keep, span].astype(F32)).astype(BF16)
                )
            total = jnp.concatenate(total, axis=0)
            out_ref[g * rows : (g + 1) * rows, cols] = dot32(turn, total).astype(BF16)


def combine_body(weigh_ref, raw_ref, out_ref):
    quarter = raw_ref.shape[1]
    half = SIDE * ROWS
    for cols in tiles(quarter, 256):
        both = dot32(weigh_ref[...], raw_ref[:, cols])
        summed = (both[:half] + both[half:]).astype(BF16)
        for c in range(SIDE):
            out_ref[:, c * quarter + cols.start : c * quarter + cols.stop] = summed[
                c * ROWS : (c + 1) * ROWS
            ]


def per_device(
    hidden_rows,
    routes,
    gate_weights,
    gate_proj,
    up_proj,
    down_proj,
    queries,
    latent_cache,
    cache_lengths,
):
    inputs = hidden_rows[0]
    width = inputs.shape[1]
    w_gate, w_up, w_down = gate_proj[0], up_proj[0], down_proj[0]
    raw_rows, quarter = SLOTS * SIDE, width // SIDE

    outgoing, weigh = local_call(
        select_body,
        [shaped(raw_rows, quarter), shaped(2 * SIDE * ROWS, raw_rows)],
        routes[0].T,
        gate_weights[0].T,
        inputs,
        flops=2 * raw_rows * SIDE * ROWS * quarter,
    )
    raw = lax.all_to_all(outgoing, "dev", 0, 0, tiled=True)
    raw, lengths, *others = lax.optimization_barrier(
        (raw, cache_lengths[0], swap_sections(w_gate), swap_sections(w_up), swap_sections(w_down))
    )
    attn_out = attention(queries[0], latent_cache[0], lengths)
    block = local_call(arrive_body, [shaped(SLOTS, width)], raw, flops=2 * SLOTS * SLOTS * width)[0]
    partials = []
    for gate_half, up_half, down_half in (
        others,
        (w_gate, w_up, w_down),
    ):
        gate = dot32(block, gate_half)
        upper = dot32(block, up_half)
        hidden, block = lax.optimization_barrier(
            ((jax.nn.silu(gate) * upper).astype(BF16), block)
        )
        partials += [
            dot32(hidden, down_half[:, span]).astype(BF16)
            for span in (slice(0, width // 2), slice(width // 2, width))
        ]
    leaving = local_call(
        leave_body,
        [shaped(raw_rows, quarter)],
        *partials,
        flops=2 * SLOTS * SLOTS * width,
    )[0]
    leaving, attn_out = lax.optimization_barrier((leaving, attn_out))
    back = lax.all_to_all(leaving, "dev", 0, 0, tiled=True)
    moe_out = local_call(
        combine_body,
        [shaped(ROWS, width)],
        weigh,
        back,
        flops=4 * raw_rows * SIDE * ROWS * quarter,
    )[0]
    return (moe_out[None], attn_out[None])


def solution(mesh):
    return jax.shard_map(
        per_device,
        mesh=mesh,
        in_specs=(
            P("section", "dev", None),
            P("section", "dev", None),
            P("section", "dev", None),
            P("dev", None, "section"),
            P("dev", None, "section"),
            P("dev", "section", None),
            P("section", "dev", None, None),
            P("section", "dev", None, None),
            P("section", "dev"),
        ),
        out_specs=(P("section", "dev", None), P("section", "dev", None, None)),
        check_vma=False,
    )
```

```python
import jax
import jax.numpy as jnp
from jax import lax
from jax.experimental import pallas as pl
from jax.experimental.pallas import tpu as pltpu
from jax.sharding import PartitionSpec as P

LAT = 512
SIDE = 4
CAP = 4
ROWS = 16
TOP = 8
SLOTS = SIDE**3 * CAP
BF16 = jnp.bfloat16
F32 = jnp.float32
I32 = jnp.int32

qk_scale = 192.0 ** (-0.5)

def swap_sections(value):
    return lax.ppermute(value, "section", [(0, 1), (1, 0)])


def dot32(left, right):
    return jnp.dot(left, right, preferred_element_type=F32)


def attention_body(lengths_ref, queries_ref, cache_ref, out_ref):
    for r in range(queries_ref.shape[0]):
        heads = queries_ref[r].astype(F32).T.astype(BF16)
        scores = dot32(heads, cache_ref[r]) * qk_scale
        valid = iota(scores.shape, 1) < lengths_ref[r]
        scores = jnp.where(valid, scores, -jnp.inf)
        peak = jnp.max(scores, axis=1, keepdims=True)
        expo = jnp.where(valid, jnp.exp(scores - peak), 0.0)
        probs = expo / jnp.sum(expo, axis=1, keepdims=True)
        out_ref[r] = dot32(cache_ref[r, :LAT, :], probs.T.astype(BF16)).T.astype(BF16)


def attention(queries, cache, lengths):
    return local_call(
        attention_body,
        [jax.ShapeDtypeStruct((*queries.shape[:2], LAT), BF16)],
        lengths,
        queries.transpose(0, 2, 1),
        cache.transpose(0, 2, 1),
        flops=4 * queries.size * cache.shape[1],
        scalars=1,
    )[0]


def local_call(body, out, *operands, flops=0, scalars=0):
    specs = [
        pl.BlockSpec(memory_space=pltpu.SMEM if i < scalars else pltpu.VMEM)
        for i in range(len(operands))
    ]
    moved = sum(v.size * v.dtype.itemsize for v in operands) + sum(
        v.size * v.dtype.itemsize for v in out
    )
    return pl.pallas_call(
        body,
        out_shape=out,
        in_specs=specs,
        out_specs=[pl.BlockSpec(memory_space=pltpu.VMEM)] * len(out),
        cost_estimate=pl.CostEstimate(flops=flops, bytes_accessed=moved, transcendentals=0),
        compiler_params=pltpu.CompilerParams(vmem_limit_bytes=16 * 2**20),
    )(*operands)


def shaped(rows, width, dtype=BF16):
    return jax.ShapeDtypeStruct((rows, width), dtype)


def tiles(width, step=512):
    return [slice(lo, min(lo + step, width)) for lo in range(0, width, step)]


def iota(shape, dim):
    return lax.broadcasted_iota(I32, shape, dim)


def select_body(routes_ref, gains_ref, rows_ref, out_ref, weigh_ref):
    quarter = rows_ref.shape[1] // SIDE
    shape = (SIDE * ROWS, out_ref.shape[0])
    left, right = iota(shape, 0), iota(shape, 1)
    expert = lax.div(right, SIDE * CAP).astype(F32)
    given = jnp.concatenate([routes_ref[...].astype(F32), gains_ref[...]], axis=0)
    given = jnp.concatenate([given, jnp.zeros((2 * TOP, 128 - ROWS), F32)], axis=1)
    given = jnp.concatenate([given, jnp.zeros((128 - 2 * TOP, 128), F32)], axis=0).T[:ROWS]
    given = jnp.concatenate([given] * SIDE, axis=0)
    named = jnp.zeros(shape, F32)
    weigh = jnp.zeros(shape, F32)
    for k in range(TOP):
        match = given[:, k : k + 1] == expert
        named = jnp.where(match, 1.0, named)
        weigh = jnp.where(match, given[:, TOP + k : TOP + k + 1], weigh)
    square = (SIDE * ROWS, SIDE * ROWS)
    row, column = iota(square, 0), iota(square, 1)
    earlier = (lax.div(row, ROWS) == lax.div(column, ROWS)) & (column < row)
    position = dot32(jnp.where(earlier, 1.0, 0.0).astype(BF16), named.astype(BF16)).astype(I32)
    hit = (
        (named > 0.5)
        & (position == lax.rem(right, CAP))
        & (lax.rem(lax.div(right, CAP), SIDE) == lax.div(left, ROWS))
    )
    weigh = jnp.where(hit, weigh, 0.0)
    high = weigh.astype(BF16)
    weigh_ref[: SIDE * ROWS, :] = high
    weigh_ref[SIDE * ROWS :, :] = (weigh - high.astype(F32)).astype(BF16)
    select = jnp.where(hit, 1.0, 0.0).T.astype(BF16)
    for cols in tiles(quarter, 256):
        rows = jnp.concatenate(
            [
                rows_ref[:, c * quarter + cols.start : c * quarter + cols.stop]
                for c in range(SIDE)
            ],
            axis=0,
        )
        out_ref[:, cols] = dot32(select, rows).astype(BF16)


def quarters_first(transposed):
    rows = SIDE * SIDE * ROWS
    out = iota((rows, rows), 1 if transposed else 0)
    given = iota((rows, rows), 0 if transposed else 1)
    group = SIDE * SIDE * CAP
    quarter, source = lax.div(out, group), lax.div(lax.rem(out, group), CAP)
    where = (source * SIDE + quarter) * CAP + lax.rem(out, CAP)
    return jnp.where(where == given, 1.0, 0.0).astype(BF16)


def arrive_body(raw_ref, out_ref):
    quarter = raw_ref.shape[1]
    turn = quarters_first(False)
    rows, group = turn.shape[0], turn.shape[0] // SIDE
    for g in range(raw_ref.shape[0] // rows):
        for cols in tiles(quarter, 256):
            turned = dot32(turn, raw_ref[g * rows : (g + 1) * rows, cols]).astype(BF16)
            for c in range(SIDE):
                out_ref[
                    g * group : (g + 1) * group, c * quarter + cols.start : c * quarter + cols.stop
                ] = turned[c * group : (c + 1) * group]


def leave_body(*refs):
    halves = len(refs) // 2
    mine, other, out_ref = refs[:halves], refs[halves : 2 * halves], refs[-1]
    quarter = out_ref.shape[1]
    turn = quarters_first(True)
    rows, group = turn.shape[0], turn.shape[0] // SIDE
    width = mine[0].shape[1]
    for g in range(out_ref.shape[0] // rows):
        for cols in tiles(quarter, 256):
            total = []
            for c in range(SIDE):
                h, at = divmod(c * quarter + cols.start, width)
                span = slice(at, at + cols.stop - cols.start)
                keep = slice(g * group, (g + 1) * group)
                total.append(
                    (mine[h][keep, span].astype(F32) + other[h][keep, span].astype(F32)).astype(BF16)
                )
            total = jnp.concatenate(total, axis=0)
            out_ref[g * rows : (g + 1) * rows, cols] = dot32(turn, total).astype(BF16)


def combine_body(weigh_ref, raw_ref, out_ref):
    quarter = raw_ref.shape[1]
    half = SIDE * ROWS
    for cols in tiles(quarter, 256):
        both = dot32(weigh_ref[...], raw_ref[:, cols])
        summed = (both[:half] + both[half:]).astype(BF16)
        for c in range(SIDE):
            out_ref[:, c * quarter + cols.start : c * quarter + cols.stop] = summed[
                c * ROWS : (c + 1) * ROWS
            ]


def per_device(
    hidden_rows,
    routes,
    gate_weights,
    gate_proj,
    up_proj,
    down_proj,
    queries,
    latent_cache,
    cache_lengths,
):
    inputs = hidden_rows[0]
    width = inputs.shape[1]
    w_gate, w_up, w_down = gate_proj[0], up_proj[0], down_proj[0]
    raw_rows, quarter = SLOTS * SIDE, width // SIDE

    outgoing, weigh = local_call(
        select_body,
        [shaped(raw_rows, quarter), shaped(2 * SIDE * ROWS, raw_rows)],
        routes[0].T,
        gate_weights[0].T,
        inputs,
        flops=2 * raw_rows * SIDE * ROWS * quarter,
    )
    raw = lax.all_to_all(outgoing, "dev", 0, 0, tiled=True)
    raw, *others = lax.optimization_barrier(
        (raw, swap_sections(w_gate), swap_sections(w_up), swap_sections(w_down))
    )
    block = local_call(arrive_body, [shaped(SLOTS, width)], raw, flops=2 * SLOTS * SLOTS * width)[0]
    partials = []
    attn_out = None
    for gate_half, up_half, down_half in (
        others,
        (w_gate, w_up, w_down),
    ):
        gate = dot32(block, gate_half)
        upper = dot32(block, up_half)
        hidden = (jax.nn.silu(gate) * upper).astype(BF16)
        hidden, block, lengths = lax.optimization_barrier((hidden, block, cache_lengths[0]))
        if attn_out is None:
            attn_out = attention(queries[0], latent_cache[0], lengths)
            block, attn_out = lax.optimization_barrier((block, attn_out))
        partials += [
            dot32(hidden, down_half[:, span]).astype(BF16)
            for span in (slice(0, width // 2), slice(width // 2, width))
        ]
    leaving = local_call(
        leave_body,
        [shaped(raw_rows, quarter)],
        *partials,
        flops=2 * SLOTS * SLOTS * width,
    )[0]
    back = lax.all_to_all(leaving, "dev", 0, 0, tiled=True)
    moe_out = local_call(
        combine_body,
        [shaped(ROWS, width)],
        weigh,
        back,
        flops=4 * raw_rows * SIDE * ROWS * quarter,
    )[0]
    return (moe_out[None], attn_out[None])


def solution(mesh):
    return jax.shard_map(
        per_device,
        mesh=mesh,
        in_specs=(
            P("section", "dev", None),
            P("section", "dev", None),
            P("section", "dev", None),
            P("dev", None, "section"),
            P("dev", None, "section"),
            P("dev", "section", None),
            P("section", "dev", None, None),
            P("section", "dev", None, None),
            P("section", "dev"),
        ),
        out_specs=(P("section", "dev", None), P("section", "dev", None, None)),
        check_vma=False,
    )
```

```python
import jax
import jax.numpy as jnp
from jax import lax
from jax.experimental import pallas as pl
from jax.experimental.pallas import tpu as pltpu
from jax.sharding import PartitionSpec as P

LAT = 512
SIDE = 4
CAP = 4
ROWS = 16
TOP = 8
SLOTS = SIDE**3 * CAP
BF16 = jnp.bfloat16
F32 = jnp.float32
I32 = jnp.int32

qk_scale = 192.0 ** (-0.5)

def swap_sections(value):
    return lax.ppermute(value, "section", [(0, 1), (1, 0)])


def dot32(left, right):
    return jnp.dot(left, right, preferred_element_type=F32)


def attention_body(lengths_ref, queries_ref, cache_ref, out_ref):
    requests = range(queries_ref.shape[0])
    heads = [queries_ref[r].astype(F32).T.astype(BF16) for r in requests]
    scores = [dot32(heads[r], cache_ref[r]) for r in requests]
    expos = []
    for r in requests:
        valid = iota(scores[r].shape, 1) < lengths_ref[r]
        used = jnp.where(valid, scores[r], -jnp.inf)
        expos.append(jnp.exp((used - jnp.max(used, axis=1, keepdims=True)) * qk_scale))
    for r in requests:
        summed = lax.dot_general(
            expos[r].astype(BF16),
            cache_ref[r, :LAT, :],
            (((1,), (1,)), ((), ())),
            preferred_element_type=F32,
        )
        out_ref[r] = (summed / jnp.sum(expos[r], axis=1, keepdims=True)).astype(BF16)


def attention(queries, cache, lengths):
    return local_call(
        attention_body,
        [jax.ShapeDtypeStruct((*queries.shape[:2], LAT), BF16)],
        lengths,
        queries.transpose(0, 2, 1),
        cache.transpose(0, 2, 1),
        flops=4 * queries.size * cache.shape[1],
        scalars=1,
    )[0]


def local_call(body, out, *operands, flops=0, scalars=0):
    specs = [
        pl.BlockSpec(memory_space=pltpu.SMEM if i < scalars else pltpu.VMEM)
        for i in range(len(operands))
    ]
    moved = sum(v.size * v.dtype.itemsize for v in operands) + sum(
        v.size * v.dtype.itemsize for v in out
    )
    return pl.pallas_call(
        body,
        out_shape=out,
        in_specs=specs,
        out_specs=[pl.BlockSpec(memory_space=pltpu.VMEM)] * len(out),
        cost_estimate=pl.CostEstimate(flops=flops, bytes_accessed=moved, transcendentals=0),
        compiler_params=pltpu.CompilerParams(vmem_limit_bytes=16 * 2**20),
    )(*operands)


def shaped(rows, width, dtype=BF16):
    return jax.ShapeDtypeStruct((rows, width), dtype)


def tiles(width, step=512):
    return [slice(lo, min(lo + step, width)) for lo in range(0, width, step)]


def iota(shape, dim):
    return lax.broadcasted_iota(I32, shape, dim)


def select_body(routes_ref, gains_ref, rows_ref, out_ref, weigh_ref):
    quarter = rows_ref.shape[1] // SIDE
    shape = (SIDE * ROWS, out_ref.shape[0])
    left, right = iota(shape, 0), iota(shape, 1)
    expert = lax.div(right, SIDE * CAP).astype(F32)
    given = jnp.concatenate([routes_ref[...].astype(F32), gains_ref[...]], axis=0)
    given = jnp.concatenate([given, jnp.zeros((2 * TOP, 128 - ROWS), F32)], axis=1)
    given = jnp.concatenate([given, jnp.zeros((128 - 2 * TOP, 128), F32)], axis=0).T[:ROWS]
    given = jnp.concatenate([given] * SIDE, axis=0)
    named = jnp.zeros(shape, F32)
    weigh = jnp.zeros(shape, F32)
    for k in range(TOP):
        match = given[:, k : k + 1] == expert
        named = jnp.where(match, 1.0, named)
        weigh = jnp.where(match, given[:, TOP + k : TOP + k + 1], weigh)
    square = (SIDE * ROWS, SIDE * ROWS)
    row, column = iota(square, 0), iota(square, 1)
    earlier = (lax.div(row, ROWS) == lax.div(column, ROWS)) & (column < row)
    position = dot32(jnp.where(earlier, 1.0, 0.0).astype(BF16), named.astype(BF16)).astype(I32)
    hit = (
        (named > 0.5)
        & (position == lax.rem(right, CAP))
        & (lax.rem(lax.div(right, CAP), SIDE) == lax.div(left, ROWS))
    )
    weigh = jnp.where(hit, weigh, 0.0)
    high = weigh.astype(BF16)
    weigh_ref[: SIDE * ROWS, :] = high
    weigh_ref[SIDE * ROWS :, :] = (weigh - high.astype(F32)).astype(BF16)
    select = jnp.where(hit, 1.0, 0.0).T.astype(BF16)
    for cols in tiles(quarter, 256):
        rows = jnp.concatenate(
            [
                rows_ref[:, c * quarter + cols.start : c * quarter + cols.stop]
                for c in range(SIDE)
            ],
            axis=0,
        )
        out_ref[:, cols] = dot32(select, rows).astype(BF16)


def quarters_first(transposed):
    rows = SIDE * SIDE * ROWS
    out = iota((rows, rows), 1 if transposed else 0)
    given = iota((rows, rows), 0 if transposed else 1)
    group = SIDE * SIDE * CAP
    quarter, source = lax.div(out, group), lax.div(lax.rem(out, group), CAP)
    where = (source * SIDE + quarter) * CAP + lax.rem(out, CAP)
    return jnp.where(where == given, 1.0, 0.0).astype(BF16)


def arrive_body(raw_ref, out_ref):
    quarter = raw_ref.shape[1]
    turn = quarters_first(False)
    rows, group = turn.shape[0], turn.shape[0] // SIDE
    for g in range(raw_ref.shape[0] // rows):
        for cols in tiles(quarter, 256):
            turned = dot32(turn, raw_ref[g * rows : (g + 1) * rows, cols]).astype(BF16)
            for c in range(SIDE):
                out_ref[
                    g * group : (g + 1) * group, c * quarter + cols.start : c * quarter + cols.stop
                ] = turned[c * group : (c + 1) * group]


def leave_body(*refs):
    halves = len(refs) // 2
    mine, other, out_ref = refs[:halves], refs[halves : 2 * halves], refs[-1]
    quarter = out_ref.shape[1]
    turn = quarters_first(True)
    rows, group = turn.shape[0], turn.shape[0] // SIDE
    width = mine[0].shape[1]
    for g in range(out_ref.shape[0] // rows):
        for cols in tiles(quarter, 256):
            total = []
            for c in range(SIDE):
                h, at = divmod(c * quarter + cols.start, width)
                span = slice(at, at + cols.stop - cols.start)
                keep = slice(g * group, (g + 1) * group)
                total.append(
                    (mine[h][keep, span].astype(F32) + other[h][keep, span].astype(F32)).astype(BF16)
                )
            total = jnp.concatenate(total, axis=0)
            out_ref[g * rows : (g + 1) * rows, cols] = dot32(turn, total).astype(BF16)


def combine_body(weigh_ref, raw_ref, out_ref):
    quarter = raw_ref.shape[1]
    half = SIDE * ROWS
    for cols in tiles(quarter, 256):
        both = dot32(weigh_ref[...], raw_ref[:, cols])
        summed = (both[:half] + both[half:]).astype(BF16)
        for c in range(SIDE):
            out_ref[:, c * quarter + cols.start : c * quarter + cols.stop] = summed[
                c * ROWS : (c + 1) * ROWS
            ]


def per_device(
    hidden_rows,
    routes,
    gate_weights,
    gate_proj,
    up_proj,
    down_proj,
    queries,
    latent_cache,
    cache_lengths,
):
    inputs = hidden_rows[0]
    width = inputs.shape[1]
    w_gate, w_up, w_down = gate_proj[0], up_proj[0], down_proj[0]
    raw_rows, quarter = SLOTS * SIDE, width // SIDE

    outgoing, weigh = local_call(
        select_body,
        [shaped(raw_rows, quarter), shaped(2 * SIDE * ROWS, raw_rows)],
        routes[0].T,
        gate_weights[0].T,
        inputs,
        flops=2 * raw_rows * SIDE * ROWS * quarter,
    )
    raw = lax.all_to_all(outgoing, "dev", 0, 0, tiled=True)
    raw, *others = lax.optimization_barrier(
        (raw, swap_sections(w_gate), swap_sections(w_up), swap_sections(w_down))
    )
    block = local_call(arrive_body, [shaped(SLOTS, width)], raw, flops=2 * SLOTS * SLOTS * width)[0]
    partials = []
    attn_out = None
    for gate_half, up_half, down_half in (
        others,
        (w_gate, w_up, w_down),
    ):
        gate = dot32(block, gate_half)
        upper = dot32(block, up_half)
        hidden = (jax.nn.silu(gate) * upper).astype(BF16)
        hidden, block, lengths = lax.optimization_barrier((hidden, block, cache_lengths[0]))
        if attn_out is None:
            attn_out = attention(queries[0], latent_cache[0], lengths)
            block, attn_out = lax.optimization_barrier((block, attn_out))
        partials += [
            dot32(hidden, down_half[:, span]).astype(BF16)
            for span in (slice(0, width // 2), slice(width // 2, width))
        ]
    leaving = local_call(
        leave_body,
        [shaped(raw_rows, quarter)],
        *partials,
        flops=2 * SLOTS * SLOTS * width,
    )[0]
    back = lax.all_to_all(leaving, "dev", 0, 0, tiled=True)
    moe_out = local_call(
        combine_body,
        [shaped(ROWS, width)],
        weigh,
        back,
        flops=4 * raw_rows * SIDE * ROWS * quarter,
    )[0]
    return (moe_out[None], attn_out[None])


def solution(mesh):
    return jax.shard_map(
        per_device,
        mesh=mesh,
        in_specs=(
            P("section", "dev", None),
            P("section", "dev", None),
            P("section", "dev", None),
            P("dev", None, "section"),
            P("dev", None, "section"),
            P("dev", "section", None),
            P("section", "dev", None, None),
            P("section", "dev", None, None),
            P("section", "dev"),
        ),
        out_specs=(P("section", "dev", None), P("section", "dev", None, None)),
        check_vma=False,
    )
```

```python
import jax
import jax.numpy as jnp
from jax import lax
from jax.experimental import pallas as pl
from jax.experimental.pallas import tpu as pltpu
from jax.sharding import PartitionSpec as P

LAT = 512
SIDE = 4
CAP = 4
ROWS = 16
TOP = 8
SLOTS = SIDE**3 * CAP
BF16 = jnp.bfloat16
F32 = jnp.float32
I32 = jnp.int32

qk_scale = 192.0 ** (-0.5)

def swap_sections(value):
    return lax.ppermute(value, "section", [(0, 1), (1, 0)])


def dot32(left, right):
    return jnp.dot(left, right, preferred_element_type=F32)


def attention_body(lengths_ref, queries_ref, cache_ref, out_ref):
    requests = range(queries_ref.shape[0])
    scores = [
        lax.dot_general(
            queries_ref[r], cache_ref[r], (((0,), (0,)), ((), ())), preferred_element_type=F32
        )
        for r in requests
    ]
    expos = []
    for r in requests:
        valid = iota(scores[r].shape, 1) < lengths_ref[r]
        used = jnp.where(valid, scores[r], -jnp.inf)
        expos.append(jnp.exp((used - jnp.max(used, axis=1, keepdims=True)) * qk_scale))
    for r in requests:
        summed = lax.dot_general(
            expos[r].astype(BF16),
            cache_ref[r, :LAT, :],
            (((1,), (1,)), ((), ())),
            preferred_element_type=F32,
        )
        out_ref[r] = (summed / jnp.sum(expos[r], axis=1, keepdims=True)).astype(BF16)


def attention(queries, cache, lengths):
    return local_call(
        attention_body,
        [jax.ShapeDtypeStruct((*queries.shape[:2], LAT), BF16)],
        lengths,
        queries.transpose(0, 2, 1),
        cache.transpose(0, 2, 1),
        flops=4 * queries.size * cache.shape[1],
        scalars=1,
    )[0]


def local_call(body, out, *operands, flops=0, scalars=0):
    specs = [
        pl.BlockSpec(memory_space=pltpu.SMEM if i < scalars else pltpu.VMEM)
        for i in range(len(operands))
    ]
    moved = sum(v.size * v.dtype.itemsize for v in operands) + sum(
        v.size * v.dtype.itemsize for v in out
    )
    return pl.pallas_call(
        body,
        out_shape=out,
        in_specs=specs,
        out_specs=[pl.BlockSpec(memory_space=pltpu.VMEM)] * len(out),
        cost_estimate=pl.CostEstimate(flops=flops, bytes_accessed=moved, transcendentals=0),
        compiler_params=pltpu.CompilerParams(vmem_limit_bytes=16 * 2**20),
    )(*operands)


def shaped(rows, width, dtype=BF16):
    return jax.ShapeDtypeStruct((rows, width), dtype)


def tiles(width, step=512):
    return [slice(lo, min(lo + step, width)) for lo in range(0, width, step)]


def iota(shape, dim):
    return lax.broadcasted_iota(I32, shape, dim)


def select_body(routes_ref, gains_ref, rows_ref, out_ref, weigh_ref):
    quarter = rows_ref.shape[1] // SIDE
    shape = (SIDE * ROWS, out_ref.shape[0])
    left, right = iota(shape, 0), iota(shape, 1)
    expert = lax.div(right, SIDE * CAP).astype(F32)
    given = jnp.concatenate([routes_ref[...].astype(F32), gains_ref[...]], axis=0)
    given = jnp.concatenate([given, jnp.zeros((2 * TOP, 128 - ROWS), F32)], axis=1)
    given = jnp.concatenate([given, jnp.zeros((128 - 2 * TOP, 128), F32)], axis=0).T[:ROWS]
    given = jnp.concatenate([given] * SIDE, axis=0)
    named = jnp.zeros(shape, F32)
    weigh = jnp.zeros(shape, F32)
    for k in range(TOP):
        match = given[:, k : k + 1] == expert
        named = jnp.where(match, 1.0, named)
        weigh = jnp.where(match, given[:, TOP + k : TOP + k + 1], weigh)
    square = (SIDE * ROWS, SIDE * ROWS)
    row, column = iota(square, 0), iota(square, 1)
    earlier = (lax.div(row, ROWS) == lax.div(column, ROWS)) & (column < row)
    position = dot32(jnp.where(earlier, 1.0, 0.0).astype(BF16), named.astype(BF16)).astype(I32)
    hit = (
        (named > 0.5)
        & (position == lax.rem(right, CAP))
        & (lax.rem(lax.div(right, CAP), SIDE) == lax.div(left, ROWS))
    )
    weigh = jnp.where(hit, weigh, 0.0)
    high = weigh.astype(BF16)
    weigh_ref[: SIDE * ROWS, :] = high
    weigh_ref[SIDE * ROWS :, :] = (weigh - high.astype(F32)).astype(BF16)
    select = jnp.where(hit, 1.0, 0.0).T.astype(BF16)
    for cols in tiles(quarter, 256):
        rows = jnp.concatenate(
            [
                rows_ref[:, c * quarter + cols.start : c * quarter + cols.stop]
                for c in range(SIDE)
            ],
            axis=0,
        )
        out_ref[:, cols] = dot32(select, rows).astype(BF16)


def quarters_first(transposed):
    rows = SIDE * SIDE * ROWS
    out = iota((rows, rows), 1 if transposed else 0)
    given = iota((rows, rows), 0 if transposed else 1)
    group = SIDE * SIDE * CAP
    quarter, source = lax.div(out, group), lax.div(lax.rem(out, group), CAP)
    where = (source * SIDE + quarter) * CAP + lax.rem(out, CAP)
    return jnp.where(where == given, 1.0, 0.0).astype(BF16)


def arrive_body(raw_ref, out_ref):
    quarter = raw_ref.shape[1]
    turn = quarters_first(False)
    rows, group = turn.shape[0], turn.shape[0] // SIDE
    for g in range(raw_ref.shape[0] // rows):
        for cols in tiles(quarter, 256):
            turned = dot32(turn, raw_ref[g * rows : (g + 1) * rows, cols]).astype(BF16)
            for c in range(SIDE):
                out_ref[
                    g * group : (g + 1) * group, c * quarter + cols.start : c * quarter + cols.stop
                ] = turned[c * group : (c + 1) * group]


def leave_body(*refs):
    halves = len(refs) // 2
    mine, other, out_ref = refs[:halves], refs[halves : 2 * halves], refs[-1]
    quarter = out_ref.shape[1]
    turn = quarters_first(True)
    rows, group = turn.shape[0], turn.shape[0] // SIDE
    width = mine[0].shape[1]
    for g in range(out_ref.shape[0] // rows):
        for cols in tiles(quarter, 256):
            total = []
            for c in range(SIDE):
                h, at = divmod(c * quarter + cols.start, width)
                span = slice(at, at + cols.stop - cols.start)
                keep = slice(g * group, (g + 1) * group)
                total.append(
                    (mine[h][keep, span].astype(F32) + other[h][keep, span].astype(F32)).astype(BF16)
                )
            total = jnp.concatenate(total, axis=0)
            out_ref[g * rows : (g + 1) * rows, cols] = dot32(turn, total).astype(BF16)


def combine_body(weigh_ref, raw_ref, out_ref):
    quarter = raw_ref.shape[1]
    half = SIDE * ROWS
    for cols in tiles(quarter, 256):
        both = dot32(weigh_ref[...], raw_ref[:, cols])
        summed = (both[:half] + both[half:]).astype(BF16)
        for c in range(SIDE):
            out_ref[:, c * quarter + cols.start : c * quarter + cols.stop] = summed[
                c * ROWS : (c + 1) * ROWS
            ]


def per_device(
    hidden_rows,
    routes,
    gate_weights,
    gate_proj,
    up_proj,
    down_proj,
    queries,
    latent_cache,
    cache_lengths,
):
    inputs = hidden_rows[0]
    width = inputs.shape[1]
    w_gate, w_up, w_down = gate_proj[0], up_proj[0], down_proj[0]
    raw_rows, quarter = SLOTS * SIDE, width // SIDE

    outgoing, weigh = local_call(
        select_body,
        [shaped(raw_rows, quarter), shaped(2 * SIDE * ROWS, raw_rows)],
        routes[0].T,
        gate_weights[0].T,
        inputs,
        flops=2 * raw_rows * SIDE * ROWS * quarter,
    )
    raw = lax.all_to_all(outgoing, "dev", 0, 0, tiled=True)
    raw, *others = lax.optimization_barrier(
        (raw, swap_sections(w_gate), swap_sections(w_up), swap_sections(w_down))
    )
    block = local_call(arrive_body, [shaped(SLOTS, width)], raw, flops=2 * SLOTS * SLOTS * width)[0]
    partials = []
    attn_out = None
    for gate_half, up_half, down_half in (
        others,
        (w_gate, w_up, w_down),
    ):
        gate = dot32(block, gate_half)
        upper = dot32(block, up_half)
        hidden = (jax.nn.silu(gate) * upper).astype(BF16)
        hidden, block, lengths = lax.optimization_barrier((hidden, block, cache_lengths[0]))
        if attn_out is None:
            attn_out = attention(queries[0], latent_cache[0], lengths)
            block, attn_out = lax.optimization_barrier((block, attn_out))
        partials += [
            dot32(hidden, down_half[:, span]).astype(BF16)
            for span in (slice(0, width // 2), slice(width // 2, width))
        ]
    leaving = local_call(
        leave_body,
        [shaped(raw_rows, quarter)],
        *partials,
        flops=2 * SLOTS * SLOTS * width,
    )[0]
    back = lax.all_to_all(leaving, "dev", 0, 0, tiled=True)
    moe_out = local_call(
        combine_body,
        [shaped(ROWS, width)],
        weigh,
        back,
        flops=4 * raw_rows * SIDE * ROWS * quarter,
    )[0]
    return (moe_out[None], attn_out[None])


def solution(mesh):
    return jax.shard_map(
        per_device,
        mesh=mesh,
        in_specs=(
            P("section", "dev", None),
            P("section", "dev", None),
            P("section", "dev", None),
            P("dev", None, "section"),
            P("dev", None, "section"),
            P("dev", "section", None),
            P("section", "dev", None, None),
            P("section", "dev", None, None),
            P("section", "dev"),
        ),
        out_specs=(P("section", "dev", None), P("section", "dev", None, None)),
        check_vma=False,
    )
```
